32 devices in a mesh: groups: 2 (over y), tm: 4 (over z), space: 4 (over x, core).
Axes of the slice: x: 2, y: 2, z: 4, core: 2. Of those that a mesh axis runs over, the one named last changes fastest.
Arguments:
- video_tokens: bfloat16 [2, 8, 512, 1024], P('groups', 'tm', 'space'), parts along dimension 0, may hold values from -8 to 8
- cotangent: bfloat16 [2, 8, 512, 1024], P('groups', 'tm', 'space'), parts along dimension 0, may hold values from -6 to 6
- time_in: bfloat16 [1024, 1536], replicated, may hold values from -0.21875 to 0.21875
- time_out: bfloat16 [1024, 512], replicated, may hold values from -0.25 to 0.25
- space_in: bfloat16 [1024, 1536], replicated, may hold values from -0.21875 to 0.21875
- space_out: bfloat16 [1024, 512], replicated, may hold values from -0.25 to 0.25
- block_mask: int32 [16, 9], replicated, may hold values 0 or 1
Outputs:
- block_out: bfloat16 [2, 8, 512, 1024], P('groups', 'tm', 'space'), parts along dimension 0
- tokens_grad: bfloat16 [2, 8, 512, 1024], P('groups', 'tm', 'space'), parts along dimension 0
- time_in_grad: float32 [2048, 1536], P(('groups', 'tm', 'space')), parts along dimension 0
- time_out_grad: float32 [2048, 512], P(('groups', 'tm', 'space')), parts along dimension 0
- space_in_grad: float32 [2048, 1536], P(('groups', 'tm', 'space')), parts along dimension 0
- space_out_grad: float32 [2048, 512], P(('groups', 'tm', 'space')), parts along dimension 0
The draws below stay inside these ranges and needn't reach their ends.
There are 2 independent parts, one for each index of `groups`. The reference program is written for one: setup_inputs(seed, part) draws one part's arguments, and reference() takes and returns one part's arrays. A program takes and returns all parts, laid end to end along the dimension named above; an argument that names none is the same for every part. Nothing has to cross between parts.
Inputs may be any that keep to these rules, and one draw needn't show every extreme that they name: block_mask[r, j] = 1 lets patch row r attend to patch row r + j - 4 of the same frame; rows outside the frame are never attended and every row attends to itself.
All inputs are finite; a program needn't handle non-finite values.
Results may differ from the reference program's by a relative error of at most 0.017.
Values may be sent and summed in bfloat16 or wider, within the bound.
A program may use at most 128 MiB of HBM per device.

```python
import jax
import jax.numpy as jnp
from jax import lax

D = 1024
HEADS = 8
HEAD = 64
COLS = 32
CLIPS = 1
INNER = 512
SPAN = 9
FRAMES = 8
PATCH_ROWS = 16
FRAME_TOKENS = 512


def draw_video_tokens(key, part):
    key = jax.random.fold_in(key, 11)
    full_shape = (CLIPS, FRAMES, FRAME_TOKENS, D)
    return jnp.clip(jax.random.normal(key, full_shape, jnp.float32), -6.0, 6.0).astype(jnp.bfloat16)


def draw_time_in(key, part):
    key = jax.random.fold_in(key, 21)
    return (jnp.clip(jax.random.normal(key, (D, 3 * INNER), jnp.float32), -6.0, 6.0) * D ** (-0.5)).astype(jnp.bfloat16)


def draw_space_in(key, part):
    key = jax.random.fold_in(key, 31)
    return (jnp.clip(jax.random.normal(key, (D, 3 * INNER), jnp.float32), -6.0, 6.0) * D ** (-0.5)).astype(jnp.bfloat16)


def touch_ends(drawn, own_key, smallest, largest):
    longest = drawn.shape.index(max(drawn.shape))
    spots = []
    for shift in (0, 1):
        where = [jax.random.randint(jax.random.fold_in(own_key, axis), (), 0, length) for axis, length in enumerate(drawn.shape)]
        where[longest] = (where[longest] + shift) % drawn.shape[longest]
        spots.append(tuple(where))
    return drawn.at[spots[0]].set(smallest).at[spots[1]].set(largest)


def spiked(result, own_key, source, target, parts, factor):
    def block_of(axis_at):
        return (jnp.arange(result.shape[axis_at]) // (result.shape[axis_at] // parts)).reshape((-1,) + (1,) * (result.ndim - 1 - axis_at))

    one_side = jax.random.permutation(own_key, parts)[block_of(target)]
    far = (block_of(target) + parts // 2) % parts
    return jnp.where((block_of(source) == one_side) | (block_of(source) == far), factor * result, result)


def block_scale(own_key, dims, shards, smallest, top_value):
    level = 1.0
    for dim, parts in shards:
        draws = jax.random.uniform(jax.random.fold_in(jax.random.fold_in(own_key, 6), dim), (parts,), jnp.float32, smallest / len(shards), top_value / len(shards))
        level = level * jnp.repeat(jnp.exp(draws), dims[dim] // parts).reshape((-1,) + (1,) * (len(dims) - 1 - dim))
    return level


def gaussian(key, dims, scale, most, shards=(), held_as=jnp.bfloat16):
    values = jax.random.normal(key, dims, jnp.float32) * scale
    if len(shards) > 0:
        values = block_scale(key, dims, shards, -0.22, 0.18) * values
    return jnp.clip(values, min=-most, max=most).astype(held_as)


def gaussian_with(own_key, extent, width, limit, cuts, heavy, kind=jnp.bfloat16):
    result = width * jax.random.normal(own_key, extent, jnp.float32)
    if cuts:
        result = result * block_scale(own_key, extent, cuts, -0.22, 0.18)
    return jnp.clip(spiked(result, jax.random.fold_in(own_key, 3), *heavy), -limit, limit).astype(kind)


def setup_inputs(seed: int = 0, part: int = 0) -> dict:
    key_of = jax.random.split(jax.random.key(seed), 8)
    part_splits = jax.random.split(jax.random.fold_in(key_of[7], part), 8)
    return {
        "video_tokens": draw_video_tokens(jax.random.fold_in(jax.random.fold_in(key_of[7], part), 71), part),
        "cotangent": gaussian_with(part_splits[1], (CLIPS, FRAMES, FRAME_TOKENS, D), 1.0, 6.0, ((1, 4), (2, 4)), (1, 3, 4, 2.0)),
        "time_in": draw_time_in(jax.random.fold_in(key_of[7], 71), part),
        "time_out": gaussian(key_of[3], (D, INNER), INNER ** -0.5, 0.25),
        "space_in": draw_space_in(jax.random.fold_in(key_of[7], 71), part),
        "space_out": gaussian(key_of[5], (D, INNER), INNER ** -0.5, 0.25),
        "block_mask": touch_ends((jax.random.randint(key_of[6], (PATCH_ROWS, SPAN), 0, 4) < 3).astype(jnp.int32), jax.random.fold_in(key_of[6], 1), 0, 1),
    }


EPSILON = 1e-05

def layer_norm(values):
    center = values - lax.optimization_barrier(jnp.mean(values, axis=-1, keepdims=True))
    variance = lax.optimization_barrier(jnp.mean(center * center, axis=-1, keepdims=True))
    inverse = lax.rsqrt(variance + EPSILON)
    return (center * inverse, inverse)

def norm_back(normed, inverse, upstream):
    first = lax.optimization_barrier(jnp.mean(upstream, axis=-1, keepdims=True))
    second = lax.optimization_barrier(jnp.mean(upstream * normed, axis=-1, keepdims=True))
    return inverse * (upstream - first - normed * second)

def rounded(values):
    return lax.optimization_barrier(values.astype(jnp.bfloat16)).astype(jnp.float32)

def row_mask(query_rows, key_rows, block_mask):
    total = block_mask.shape[0]
    span = block_mask.shape[1]
    reach = (span - 1) // 2
    table = jnp.arange(total, dtype=jnp.int32)
    picks = (query_rows[:, None] == table[None, :]).astype(jnp.int32)
    row_vals = lax.optimization_barrier(jnp.sum(picks[:, :, None] * block_mask[None, :, :], axis=1))
    offsets = key_rows[None, :] - query_rows[:, None] + reach
    spots = jnp.arange(span, dtype=jnp.int32)
    picked = lax.optimization_barrier(jnp.sum((offsets[:, :, None] == spots[None, None, :]).astype(jnp.int32) * row_vals[:, None, :], axis=2))
    query_ok = (query_rows >= 0) & (query_rows < total)
    key_ok = (key_rows >= 0) & (key_rows < total)
    same = key_rows[None, :] == query_rows[:, None]
    return ((picked == 1) | same) & query_ok[:, None] & key_ok[None, :]

def token_mask(query_rows, key_rows, block_mask):
    rows_ok = row_mask(query_rows, key_rows, block_mask)
    return jnp.repeat(jnp.repeat(rows_ok, COLS, axis=0), COLS, axis=1)

def time_probs(queries, keys, scale):
    scores = jnp.einsum('cfphe,cgphe->cphfg', queries.astype(jnp.float32), keys.astype(jnp.float32)) * scale
    peak = lax.optimization_barrier(jnp.max(scores, axis=-1, keepdims=True))
    total = jnp.log(lax.optimization_barrier(jnp.sum(jnp.exp(scores - peak), axis=-1, keepdims=True))) + peak
    return jnp.exp(scores - total)

def time_forward(queries, keys, values, scale):
    weights = rounded(time_probs(queries, keys, scale))
    return jnp.einsum('cphfg,cgphe->cfphe', weights, values.astype(jnp.float32)).astype(jnp.bfloat16)

def time_backward(queries, keys, values, upstream, scale):
    probs = time_probs(queries, keys, scale)
    weights = rounded(probs)
    incoming = upstream.astype(jnp.float32)
    slopes = jnp.einsum('cfphe,cgphe->cphfg', incoming, values.astype(jnp.float32))
    center = lax.optimization_barrier(jnp.sum(probs * slopes, axis=-1, keepdims=True))
    shares = rounded(probs * (slopes - center))
    grad_queries = (jnp.einsum('cphfg,cgphe->cfphe', shares, keys.astype(jnp.float32)) * scale).astype(jnp.bfloat16)
    grad_keys = (jnp.einsum('cphfg,cfphe->cgphe', shares, queries.astype(jnp.float32)) * scale).astype(jnp.bfloat16)
    grad_values = jnp.einsum('cphfg,cfphe->cgphe', weights, incoming).astype(jnp.bfloat16)
    return (grad_queries, grad_keys, grad_values)

def space_probs(queries, keys, allowed, scale):
    scores = jnp.einsum('qhe,khe->hqk', queries.astype(jnp.float32), keys.astype(jnp.float32)) * scale
    scores = jnp.where(allowed[None], scores, -jnp.inf)
    peak = lax.optimization_barrier(jnp.max(scores, axis=-1, keepdims=True))
    total = jnp.log(lax.optimization_barrier(jnp.sum(jnp.exp(scores - peak), axis=-1, keepdims=True))) + peak
    return jnp.where(allowed[None], jnp.exp(scores - total), 0.0)

def reference(video_tokens, cotangent, time_in, time_out, space_in, space_out, block_mask):
    inner = HEADS * HEAD
    scale = HEAD ** (-0.5)
    total_rows = CLIPS * FRAMES * FRAME_TOKENS
    inputs = video_tokens.astype(jnp.float32)
    normed_one, inverse_one = layer_norm(inputs)
    first_in = normed_one.astype(jnp.bfloat16)
    time_qkv = jnp.dot(first_in.reshape(total_rows, D), time_in, preferred_element_type=jnp.float32).astype(jnp.bfloat16)
    time_qkv = time_qkv.reshape(CLIPS, FRAMES, FRAME_TOKENS, 3, HEADS, HEAD)
    time_attn = time_forward(time_qkv[:, :, :, 0], time_qkv[:, :, :, 1], time_qkv[:, :, :, 2], scale)
    time_attn = time_attn.reshape(total_rows, inner)
    hidden = inputs + jnp.dot(time_attn, time_out.T, preferred_element_type=jnp.float32).reshape(inputs.shape)
    normed_two, inverse_two = layer_norm(hidden)
    second_in = normed_two.astype(jnp.bfloat16)
    space_qkv = jnp.dot(second_in.reshape(total_rows, D), space_in, preferred_element_type=jnp.float32).astype(jnp.bfloat16)
    frames_qkv = space_qkv.reshape(CLIPS * FRAMES, FRAME_TOKENS, 3, HEADS, HEAD)
    rows_all = jnp.arange(PATCH_ROWS, dtype=jnp.int32)
    allowed = token_mask(rows_all, rows_all, block_mask)

    def space_one(piece):
        probs = space_probs(piece[:, 0], piece[:, 1], allowed, scale)
        mixed = jnp.einsum('hqk,khe->qhe', rounded(probs), piece[:, 2].astype(jnp.float32))
        return mixed.astype(jnp.bfloat16).reshape(FRAME_TOKENS, inner)
    space_attn = lax.map(space_one, frames_qkv).reshape(total_rows, inner)
    block_out = (hidden + jnp.dot(space_attn, space_out.T, preferred_element_type=jnp.float32).reshape(inputs.shape)).astype(jnp.bfloat16)
    cotan_flat = cotangent.reshape(total_rows, D)
    upstream = cotangent.astype(jnp.float32)
    space_up = jnp.dot(cotan_flat, space_out, preferred_element_type=jnp.float32).astype(jnp.bfloat16)
    frames_up = space_up.reshape(CLIPS * FRAMES, FRAME_TOKENS, HEADS, HEAD)

    def space_back(pair):
        piece, incoming_low = pair
        queries = piece[:, 0].astype(jnp.float32)
        keys = piece[:, 1].astype(jnp.float32)
        values = piece[:, 2].astype(jnp.float32)
        probs = space_probs(piece[:, 0], piece[:, 1], allowed, scale)
        weights = rounded(probs)
        incoming = incoming_low.astype(jnp.float32)
        slopes = jnp.einsum('qhe,khe->hqk', incoming, values)
        center = lax.optimization_barrier(jnp.sum(probs * slopes, axis=-1, keepdims=True))
        shares = rounded(probs * (slopes - center))
        grad_queries = (jnp.einsum('hqk,khe->qhe', shares, keys) * scale).astype(jnp.bfloat16)
        grad_keys = (jnp.einsum('hqk,qhe->khe', shares, queries) * scale).astype(jnp.bfloat16)
        grad_values = jnp.einsum('hqk,qhe->khe', weights, incoming).astype(jnp.bfloat16)
        return jnp.concatenate([grad_queries.reshape(FRAME_TOKENS, inner), grad_keys.reshape(FRAME_TOKENS, inner), grad_values.reshape(FRAME_TOKENS, inner)], axis=-1)
    space_grads = lax.map(space_back, (frames_qkv, frames_up)).reshape(total_rows, 3 * inner)
    back_two = jnp.dot(space_grads, space_in.T, preferred_element_type=jnp.float32).reshape(inputs.shape)
    hidden_grad = upstream + norm_back(normed_two, inverse_two, back_two)
    hidden_low = hidden_grad.astype(jnp.bfloat16).reshape(total_rows, D)
    time_up = jnp.dot(hidden_low, time_out, preferred_element_type=jnp.float32).astype(jnp.bfloat16)
    time_up = time_up.reshape(CLIPS, FRAMES, FRAME_TOKENS, HEADS, HEAD)
    grads = time_backward(time_qkv[:, :, :, 0], time_qkv[:, :, :, 1], time_qkv[:, :, :, 2], time_up, scale)
    time_grads = jnp.concatenate([member.reshape(total_rows, inner) for member in grads], axis=-1)
    back_one = jnp.dot(time_grads, time_in.T, preferred_element_type=jnp.float32).reshape(inputs.shape)
    tokens_grad = (hidden_grad + norm_back(normed_one, inverse_one, back_one)).astype(jnp.bfloat16)
    time_in_grad = jnp.dot(first_in.reshape(total_rows, D).T, time_grads, preferred_element_type=jnp.float32)
    time_out_grad = jnp.dot(hidden_low.T, time_attn, preferred_element_type=jnp.float32)
    space_in_grad = jnp.dot(second_in.reshape(total_rows, D).T, space_grads, preferred_element_type=jnp.float32)
    space_out_grad = jnp.dot(cotan_flat.T, space_attn, preferred_element_type=jnp.float32)
    return (block_out, tokens_grad, time_in_grad, time_out_grad, space_in_grad, space_out_grad)
```

```python
import jax
import jax.numpy as jnp
from jax import lax
from jax.experimental import pallas as pl
from jax.experimental.pallas import tpu as pltpu
from jax.sharding import PartitionSpec as P

HEADS = 8
HEAD = 64
COLS = 32
INNER = HEADS * HEAD
SCALE = HEAD ** (-0.5)
EPSILON = 1e-05
VMEM_BYTES = 40 * 2**20
MASKED = -1e30


def layer_norm(values):
    center = values - jnp.mean(values, axis=-1, keepdims=True)
    variance = jnp.mean(center * center, axis=-1, keepdims=True)
    inverse = lax.rsqrt(variance + EPSILON)
    return (center * inverse, inverse)


def norm_back(normed, inverse, upstream):
    first = jnp.mean(upstream, axis=-1, keepdims=True)
    second = jnp.mean(upstream * normed, axis=-1, keepdims=True)
    return inverse * (upstream - first - normed * second)


def dot(left, right, left_dim, right_dim):
    return lax.dot_general(
        left, right, (((left_dim,), (right_dim,)), ((), ())), preferred_element_type=jnp.float32
    )


def head_of(array, index):
    return array[:, index * HEAD : (index + 1) * HEAD]


def softmax(queries, keys, allowed):
    scores = jnp.where(allowed, dot(queries, keys, 1, 1) * SCALE, MASKED)
    peak = jnp.max(scores, axis=-1, keepdims=True)
    raised = jnp.exp(scores - peak)
    return raised / jnp.sum(raised, axis=-1, keepdims=True)


def shares_of(probs, incoming, values):
    slopes = dot(incoming, values, 1, 1)
    center = jnp.sum(probs * slopes, axis=-1, keepdims=True)
    return (probs * (slopes - center)).astype(jnp.bfloat16)


def side_by_side(members):
    return jnp.concatenate(members, axis=-1)


def same_place(tokens, places):
    rows = lax.broadcasted_iota(jnp.int32, (tokens, tokens), 0)
    columns = lax.broadcasted_iota(jnp.int32, (tokens, tokens), 1)
    return lax.rem(rows, places) == lax.rem(columns, places)


def time_forward(places, tokens_ref, weight_ref, first_ref, qkv_ref, attn_ref):
    normed, _ = layer_norm(tokens_ref[...].astype(jnp.float32))
    first = normed.astype(jnp.bfloat16)
    first_ref[...] = first
    qkv_ref[...] = dot(first, weight_ref[...], 1, 0).astype(jnp.bfloat16)
    qkv = qkv_ref[...]
    allowed = same_place(qkv.shape[0], places)
    mixed = []
    for index in range(HEADS):
        queries, keys, values = [head_of(qkv, index + part * HEADS) for part in range(3)]
        weights = softmax(queries, keys, allowed).astype(jnp.bfloat16)
        mixed.append(dot(weights, values, 1, 0).astype(jnp.bfloat16))
    attn_ref[...] = side_by_side(mixed)


def time_backward(places, tokens_ref, qkv_ref, up_ref, weight_ref, grads_ref, back_ref):
    qkv = qkv_ref[...]
    upstream = up_ref[...]
    allowed = same_place(qkv.shape[0], places)
    grads = [[], [], []]
    for index in range(HEADS):
        queries, keys, values = [head_of(qkv, index + part * HEADS) for part in range(3)]
        incoming = head_of(upstream, index)
        probs = softmax(queries, keys, allowed)
        weights = probs.astype(jnp.bfloat16)
        shares = shares_of(probs, incoming, values)
        grads[0].append((dot(shares, keys, 1, 0) * SCALE).astype(jnp.bfloat16))
        grads[1].append((dot(shares, queries, 0, 0) * SCALE).astype(jnp.bfloat16))
        grads[2].append(dot(weights, incoming, 0, 0).astype(jnp.bfloat16))
    grads_ref[...] = side_by_side(grads[0] + grads[1] + grads[2])
    normed, inverse = layer_norm(tokens_ref[...].astype(jnp.float32))
    back = dot(grads_ref[...], weight_ref[...], 1, 1)
    back_ref[...] = norm_back(normed, inverse, back).astype(jnp.bfloat16)


def space_project(tokens_ref, attn_ref, out_ref, weight_ref, hidden_ref, second_ref, qkv_ref):
    hidden = tokens_ref[...].astype(jnp.float32) + dot(attn_ref[...], out_ref[...], 1, 1)
    hidden_ref[...] = hidden
    normed, _ = layer_norm(hidden)
    second = normed.astype(jnp.bfloat16)
    second_ref[...] = second
    qkv_ref[...] = dot(second, weight_ref[...], 1, 0).astype(jnp.bfloat16)


def space_attention(
    qkv_ref, before_ref, after_ref, up_ref, table_ref, attn_ref, query_ref, own_ref, up_out, down_out
):
    strip = qkv_ref.shape[0]
    span = table_ref.shape[1]
    rows = lax.broadcasted_iota(jnp.int32, (strip, 3 * strip), 0) // COLS
    columns = lax.broadcasted_iota(jnp.int32, (strip, 3 * strip), 1) // COLS
    offsets = columns - strip // COLS - rows + (span - 1) // 2
    picked = jnp.zeros((strip, 3 * strip), jnp.float32)
    for spot in range(span):
        picked = jnp.where(offsets == spot, table_ref[:, spot : spot + 1], picked)
    allowed = picked > 0.5
    qkv = qkv_ref[...]
    upstream = up_ref[...]
    near = jnp.concatenate([before_ref[...], qkv[:, INNER:], after_ref[...]], axis=0)
    mixed, grad_queries, grad_keys, grad_values = [], [], [], []
    for index in range(HEADS):
        queries = head_of(qkv, index)
        keys = head_of(near, index)
        values = head_of(near, index + HEADS)
        incoming = head_of(upstream, index)
        probs = softmax(queries, keys, allowed)
        weights = probs.astype(jnp.bfloat16)
        mixed.append(dot(weights, values, 1, 0).astype(jnp.bfloat16))
        shares = shares_of(probs, incoming, values)
        grad_queries.append((dot(shares, keys, 1, 0) * SCALE).astype(jnp.bfloat16))
        grad_keys.append(dot(shares, queries, 0, 0) * SCALE)
        grad_values.append(dot(weights, incoming, 0, 0))
    attn_ref[...] = side_by_side(mixed)
    query_ref[...] = side_by_side(grad_queries)
    pair = side_by_side(grad_keys + grad_values)
    up_out[...] = pair[:strip].astype(jnp.bfloat16)
    own_ref[...] = pair[strip : 2 * strip]
    down_out[...] = pair[2 * strip :].astype(jnp.bfloat16)


def hidden_backward(
    cotangent_ref, hidden_ref, query_ref, own_ref, one_ref, two_ref, weight_ref, out_ref,
    grads_ref, grad_ref, low_ref, up_ref,
):
    pair = own_ref[...] + one_ref[...].astype(jnp.float32) + two_ref[...].astype(jnp.float32)
    grads = side_by_side([query_ref[...], pair.astype(jnp.bfloat16)])
    grads_ref[...] = grads
    normed, inverse = layer_norm(hidden_ref[...])
    back = norm_back(normed, inverse, dot(grads, weight_ref[...], 1, 1))
    total = cotangent_ref[...].astype(jnp.float32) + back
    grad_ref[...] = total
    low = total.astype(jnp.bfloat16)
    low_ref[...] = low
    up_ref[...] = dot(low, out_ref[...], 1, 0).astype(jnp.bfloat16)


def whole_call(body, outs, *arrays):
    return pl.pallas_call(
        body,
        out_shape=[jax.ShapeDtypeStruct(shape, kind) for shape, kind in outs],
        compiler_params=pltpu.CompilerParams(vmem_limit_bytes=VMEM_BYTES),
    )(*arrays)


def passed_along(value, axis, steps):
    count = lax.axis_size(axis)
    leading, last = (max(0, -steps), min(count, count - steps))
    return lax.ppermute(value, axis, [(source, source + steps) for source in range(leading, last)])


def product(left, right):
    return dot(left, right, 0, 0).astype(jnp.bfloat16)


def by_owner(partial):
    rows, columns = partial.shape
    times, places = lax.axis_size("tm"), lax.axis_size("space")
    return partial.reshape(times, places, rows // (times * places), columns)


def halved(held, step):
    times, left, rows, columns = held.shape
    split = held.reshape(times, left // 2, 2, rows, columns)
    bit = lax.rem(lax.axis_index("space") // step, 2)
    keep = lax.dynamic_index_in_dim(split, bit, 2, keepdims=False)
    give = lax.dynamic_index_in_dim(split, 1 - bit, 2, keepdims=False)
    pairs = [(i, i ^ step) for i in range(lax.axis_size("space"))]
    got = lax.ppermute(give, "space", pairs)
    return (keep.astype(jnp.float32) + got.astype(jnp.float32)).astype(jnp.bfloat16)


def summed(held, step):
    while held.shape[1] > 1:
        held = halved(held, step)
        step *= 2
    held = held.reshape(held.shape[0] * held.shape[2], held.shape[3])
    return lax.psum_scatter(held, "tm", scatter_dimension=0, tiled=True).astype(jnp.float32)


def shards(video_tokens, cotangent, time_in, time_out, space_in, space_out, block_mask):
    clips, frames, strip, width = video_tokens.shape
    times = lax.axis_size("tm")
    places = strip // times
    tokens = clips * frames * strip
    low, full = jnp.bfloat16, jnp.float32

    def to_places(array):
        wide = array.reshape(clips, frames, strip, array.shape[-1])
        moved = lax.all_to_all(wide, "tm", split_axis=2, concat_axis=1, tiled=True)
        return moved.reshape(tokens, array.shape[-1])

    def to_frames(array):
        wide = array.reshape(clips, frames * times, places, array.shape[-1])
        moved = lax.all_to_all(wide, "tm", split_axis=1, concat_axis=2, tiled=True)
        return moved.reshape(tokens, array.shape[-1])

    own_tokens = video_tokens.reshape(tokens, width)
    cotan = cotangent.reshape(tokens, width)
    placed = to_places(own_tokens)
    space_up = dot(cotan, space_out, 1, 0).astype(low)

    total, span = block_mask.shape
    reach = (span - 1) // 2
    rows_dev = strip // COLS
    first_row = lax.axis_index("space") * rows_dev
    own_mask = lax.dynamic_slice_in_dim(block_mask, first_row, rows_dev, axis=0)
    spots = jnp.arange(span, dtype=jnp.int32)[None, :] - reach
    key_rows = first_row + jnp.arange(rows_dev, dtype=jnp.int32)[:, None] + spots
    table = ((own_mask == 1) | (spots == 0)) & (key_rows >= 0) & (key_rows < total)
    table = jnp.repeat(table.astype(full), COLS, axis=0)

    def time_forward_here(*refs):
        time_forward(places, *refs)

    def time_backward_here(*refs):
        time_backward(places, *refs)

    first_in, time_qkv, mixed = whole_call(
        time_forward_here,
        [((tokens, width), low), ((tokens, 3 * INNER), low), ((tokens, INNER), low)],
        placed, time_in,
    )
    time_attn = to_frames(mixed)
    hidden, second_in, space_qkv = whole_call(
        space_project,
        [((tokens, width), full), ((tokens, width), low), ((tokens, 3 * INNER), low)],
        own_tokens, time_attn, time_out, space_in,
    )
    pair = space_qkv[:, INNER:]
    before = passed_along(pair, "space", 1)
    after = passed_along(pair, "space", -1)

    def block(columns):
        return pl.BlockSpec((strip, columns), lambda frame: (frame, 0))

    space_attn, grad_queries, own_pair, up_pair, down_pair = pl.pallas_call(
        space_attention,
        grid=(clips * frames,),
        in_specs=[
            block(3 * INNER), block(2 * INNER), block(2 * INNER), block(INNER),
            pl.BlockSpec((strip, span), lambda frame: (0, 0)),
        ],
        out_specs=[
            block(INNER), block(INNER), block(2 * INNER), block(2 * INNER), block(2 * INNER)
        ],
        out_shape=[
            jax.ShapeDtypeStruct((tokens, INNER), low),
            jax.ShapeDtypeStruct((tokens, INNER), low),
            jax.ShapeDtypeStruct((tokens, 2 * INNER), full),
            jax.ShapeDtypeStruct((tokens, 2 * INNER), low),
            jax.ShapeDtypeStruct((tokens, 2 * INNER), low),
        ],
        compiler_params=pltpu.CompilerParams(vmem_limit_bytes=VMEM_BYTES),
    )(space_qkv, before, after, space_up, table)
    from_above = passed_along(up_pair, "space", -1)
    from_below = passed_along(down_pair, "space", 1)
    space_grads, hidden_grad, hidden_low, time_up = whole_call(
        hidden_backward,
        [
            ((tokens, 3 * INNER), low), ((tokens, width), full),
            ((tokens, width), low), ((tokens, INNER), low),
        ],
        cotan, hidden, grad_queries, own_pair, from_above, from_below, space_in, time_out,
    )
    early = halved(
        by_owner(
            jnp.concatenate(
                [
                    product(cotan, space_attn),
                    product(second_in, space_grads),
                    product(hidden_low, time_attn),
                ],
                axis=1,
            )
        ),
        1,
    )
    early, placed_up = lax.optimization_barrier((early, to_places(time_up)))
    time_grads, back = whole_call(
        time_backward_here,
        [((tokens, 3 * INNER), low), ((tokens, width), low)],
        placed, time_qkv, placed_up, time_in,
    )
    early = summed(early, 2)
    late = summed(halved(by_owner(product(first_in, time_grads)), 1), 2)
    block_out = (hidden + dot(space_attn, space_out, 1, 1)).astype(low)
    tokens_grad = (hidden_grad + to_frames(back).astype(full)).astype(low)
    shape = video_tokens.shape
    return (
        block_out.reshape(shape),
        tokens_grad.reshape(shape),
        late,
        early[:, 4 * INNER :],
        early[:, INNER : 4 * INNER],
        early[:, :INNER],
    )


def solution(mesh):
    return jax.shard_map(
        shards,
        mesh=mesh,
        in_specs=(
            P("groups", "tm", "space", None),
            P("groups", "tm", "space", None),
            P(),
            P(),
            P(),
            P(),
            P(),
        ),
        out_specs=(
            P("groups", "tm", "space", None),
            P("groups", "tm", "space", None),
            P(("groups", "tm", "space"), None),
            P(("groups", "tm", "space"), None),
            P(("groups", "tm", "space"), None),
            P(("groups", "tm", "space"), None),
        ),
        check_vma=False,
    )
```

```python
import jax
import jax.numpy as jnp
from jax import lax
from jax.experimental import pallas as pl
from jax.experimental.pallas import tpu as pltpu
from jax.sharding import PartitionSpec as P

HEADS = 8
HEAD = 64
COLS = 32
INNER = HEADS * HEAD
SCALE = HEAD ** (-0.5)
EPSILON = 1e-05
VMEM_BYTES = 40 * 2**20
MASKED = -1e30


def layer_norm(values):
    center = values - jnp.mean(values, axis=-1, keepdims=True)
    variance = jnp.mean(center * center, axis=-1, keepdims=True)
    inverse = lax.rsqrt(variance + EPSILON)
    return (center * inverse, inverse)


def norm_back(normed, inverse, upstream):
    first = jnp.mean(upstream, axis=-1, keepdims=True)
    second = jnp.mean(upstream * normed, axis=-1, keepdims=True)
    return inverse * (upstream - first - normed * second)


def dot(left, right, left_dim, right_dim):
    return lax.dot_general(
        left, right, (((left_dim,), (right_dim,)), ((), ())), preferred_element_type=jnp.float32
    )


def head_of(array, index):
    return array[:, index * HEAD : (index + 1) * HEAD]


def softmax(queries, keys, allowed):
    scores = jnp.where(allowed, dot(queries * SCALE, keys, 1, 1), MASKED)
    peak = jnp.max(scores, axis=-1, keepdims=True)
    raised = jnp.exp(scores - peak)
    return raised * (1.0 / jnp.sum(raised, axis=-1, keepdims=True))


def shares_of(probs, incoming, values):
    slopes = dot(incoming, values, 1, 1)
    center = jnp.sum(probs * slopes, axis=-1, keepdims=True)
    return (probs * (slopes - center)).astype(jnp.bfloat16)


def side_by_side(members):
    return jnp.concatenate(members, axis=-1)


def same_place(tokens, places):
    rows = lax.broadcasted_iota(jnp.int32, (tokens, tokens), 0)
    columns = lax.broadcasted_iota(jnp.int32, (tokens, tokens), 1)
    return lax.rem(rows, places) == lax.rem(columns, places)


def time_forward(places, tokens_ref, weight_ref, first_ref, qkv_ref, attn_ref):
    normed, _ = layer_norm(tokens_ref[...].astype(jnp.float32))
    first = normed.astype(jnp.bfloat16)
    first_ref[...] = first
    qkv_ref[...] = dot(first, weight_ref[...], 1, 0).astype(jnp.bfloat16)
    qkv = qkv_ref[...]
    allowed = same_place(qkv.shape[0], places)
    mixed = []
    for index in range(HEADS):
        queries, keys, values = [head_of(qkv, index + part * HEADS) for part in range(3)]
        weights = softmax(queries, keys, allowed).astype(jnp.bfloat16)
        mixed.append(dot(weights, values, 1, 0).astype(jnp.bfloat16))
    attn_ref[...] = side_by_side(mixed)


def time_backward(places, tokens_ref, qkv_ref, up_ref, weight_ref, grads_ref, back_ref):
    qkv = qkv_ref[...]
    upstream = up_ref[...]
    allowed = same_place(qkv.shape[0], places)
    grads = [[], [], []]
    for index in range(HEADS):
        queries, keys, values = [head_of(qkv, index + part * HEADS) for part in range(3)]
        incoming = head_of(upstream, index)
        probs = softmax(queries, keys, allowed)
        weights = probs.astype(jnp.bfloat16)
        shares = shares_of(probs, incoming, values)
        grads[0].append((dot(shares, keys, 1, 0) * SCALE).astype(jnp.bfloat16))
        grads[1].append((dot(shares, queries, 0, 0) * SCALE).astype(jnp.bfloat16))
        grads[2].append(dot(weights, incoming, 0, 0).astype(jnp.bfloat16))
    grads_ref[...] = side_by_side(grads[0] + grads[1] + grads[2])
    normed, inverse = layer_norm(tokens_ref[...].astype(jnp.float32))
    back = dot(grads_ref[...], weight_ref[...], 1, 1)
    back_ref[...] = norm_back(normed, inverse, back).astype(jnp.bfloat16)


def space_project(tokens_ref, attn_ref, out_ref, weight_ref, hidden_ref, second_ref, qkv_ref):
    hidden = tokens_ref[...].astype(jnp.float32) + dot(attn_ref[...], out_ref[...], 1, 1)
    hidden_ref[...] = hidden
    normed, _ = layer_norm(hidden)
    second = normed.astype(jnp.bfloat16)
    second_ref[...] = second
    qkv_ref[...] = dot(second, weight_ref[...], 1, 0).astype(jnp.bfloat16)


def space_attention(
    qkv_ref, before_ref, after_ref, up_ref, table_ref, attn_ref, query_ref, own_ref, up_out, down_out
):
    strip = qkv_ref.shape[0]
    span = table_ref.shape[1]
    rows = lax.broadcasted_iota(jnp.int32, (strip, 3 * strip), 0) // COLS
    columns = lax.broadcasted_iota(jnp.int32, (strip, 3 * strip), 1) // COLS
    offsets = columns - strip // COLS - rows + (span - 1) // 2
    picked = jnp.zeros((strip, 3 * strip), jnp.float32)
    for spot in range(span):
        picked = jnp.where(offsets == spot, table_ref[:, spot : spot + 1], picked)
    allowed = picked > 0.5
    qkv = qkv_ref[...]
    upstream = up_ref[...]
    near = jnp.concatenate([before_ref[...], qkv[:, INNER:], after_ref[...]], axis=0)
    mixed, grad_queries, grad_keys, grad_values = [], [], [], []
    for index in range(HEADS):
        queries = head_of(qkv, index)
        keys = head_of(near, index)
        values = head_of(near, index + HEADS)
        incoming = head_of(upstream, index)
        probs = softmax(queries, keys, allowed)
        weights = probs.astype(jnp.bfloat16)
        mixed.append(dot(weights, values, 1, 0).astype(jnp.bfloat16))
        shares = shares_of(probs, incoming, values)
        grad_queries.append((dot(shares, keys, 1, 0) * SCALE).astype(jnp.bfloat16))
        grad_keys.append(dot(shares, queries, 0, 0) * SCALE)
        grad_values.append(dot(weights, incoming, 0, 0))
    attn_ref[...] = side_by_side(mixed)
    query_ref[...] = side_by_side(grad_queries)
    pair = side_by_side(grad_keys + grad_values)
    up_out[...] = pair[:strip].astype(jnp.bfloat16)
    own_ref[...] = pair[strip : 2 * strip]
    down_out[...] = pair[2 * strip :].astype(jnp.bfloat16)


def hidden_backward(
    cotangent_ref, hidden_ref, query_ref, own_ref, one_ref, two_ref, weight_ref, out_ref,
    grads_ref, grad_ref, low_ref, up_ref,
):
    pair = own_ref[...] + one_ref[...].astype(jnp.float32) + two_ref[...].astype(jnp.float32)
    grads = side_by_side([query_ref[...], pair.astype(jnp.bfloat16)])
    grads_ref[...] = grads
    normed, inverse = layer_norm(hidden_ref[...])
    back = norm_back(normed, inverse, dot(grads, weight_ref[...], 1, 1))
    total = cotangent_ref[...].astype(jnp.float32) + back
    grad_ref[...] = total
    low = total.astype(jnp.bfloat16)
    low_ref[...] = low
    up_ref[...] = dot(low, out_ref[...], 1, 0).astype(jnp.bfloat16)


def whole_call(body, outs, *arrays):
    return pl.pallas_call(
        body,
        out_shape=[jax.ShapeDtypeStruct(shape, kind) for shape, kind in outs],
        compiler_params=pltpu.CompilerParams(vmem_limit_bytes=VMEM_BYTES),
    )(*arrays)


def passed_along(value, axis, steps):
    count = lax.axis_size(axis)
    leading, last = (max(0, -steps), min(count, count - steps))
    return lax.ppermute(value, axis, [(source, source + steps) for source in range(leading, last)])


def product(left, right):
    return dot(left, right, 0, 0).astype(jnp.bfloat16)


def by_owner(partial):
    rows, columns = partial.shape
    times, places = lax.axis_size("tm"), lax.axis_size("space")
    return partial.reshape(times, places, rows // (times * places), columns)


def halved(held, step):
    times, left, rows, columns = held.shape
    split = held.reshape(times, left // 2, 2, rows, columns)
    bit = lax.rem(lax.axis_index("space") // step, 2)
    keep = lax.dynamic_index_in_dim(split, bit, 2, keepdims=False)
    give = lax.dynamic_index_in_dim(split, 1 - bit, 2, keepdims=False)
    pairs = [(i, i ^ step) for i in range(lax.axis_size("space"))]
    got = lax.ppermute(give, "space", pairs)
    return (keep.astype(jnp.float32) + got.astype(jnp.float32)).astype(jnp.bfloat16)


def summed(held, step):
    while held.shape[1] > 1:
        held = halved(held, step)
        step *= 2
    held = held.reshape(held.shape[0] * held.shape[2], held.shape[3])
    return lax.psum_scatter(held, "tm", scatter_dimension=0, tiled=True).astype(jnp.float32)


def shards(video_tokens, cotangent, time_in, time_out, space_in, space_out, block_mask):
    clips, frames, strip, width = video_tokens.shape
    times = lax.axis_size("tm")
    places = strip // times
    tokens = clips * frames * strip
    low, full = jnp.bfloat16, jnp.float32

    def to_places(array):
        wide = array.reshape(clips, frames, strip, array.shape[-1])
        moved = lax.all_to_all(wide, "tm", split_axis=2, concat_axis=1, tiled=True)
        return moved.reshape(tokens, array.shape[-1])

    def to_frames(array):
        wide = array.reshape(clips, frames * times, places, array.shape[-1])
        moved = lax.all_to_all(wide, "tm", split_axis=1, concat_axis=2, tiled=True)
        return moved.reshape(tokens, array.shape[-1])

    own_tokens = video_tokens.reshape(tokens, width)
    cotan = cotangent.reshape(tokens, width)
    placed = to_places(own_tokens)
    space_up = dot(cotan, space_out, 1, 0).astype(low)

    total, span = block_mask.shape
    reach = (span - 1) // 2
    rows_dev = strip // COLS
    first_row = lax.axis_index("space") * rows_dev
    own_mask = lax.dynamic_slice_in_dim(block_mask, first_row, rows_dev, axis=0)
    spots = jnp.arange(span, dtype=jnp.int32)[None, :] - reach
    key_rows = first_row + jnp.arange(rows_dev, dtype=jnp.int32)[:, None] + spots
    table = ((own_mask == 1) | (spots == 0)) & (key_rows >= 0) & (key_rows < total)
    table = jnp.repeat(table.astype(full), COLS, axis=0)

    def time_forward_here(*refs):
        time_forward(places, *refs)

    def time_backward_here(*refs):
        time_backward(places, *refs)

    first_in, time_qkv, mixed = whole_call(
        time_forward_here,
        [((tokens, width), low), ((tokens, 3 * INNER), low), ((tokens, INNER), low)],
        placed, time_in,
    )
    time_attn = to_frames(mixed)
    hidden, second_in, space_qkv = whole_call(
        space_project,
        [((tokens, width), full), ((tokens, width), low), ((tokens, 3 * INNER), low)],
        own_tokens, time_attn, time_out, space_in,
    )
    pair = space_qkv[:, INNER:]
    before = passed_along(pair, "space", 1)
    after = passed_along(pair, "space", -1)

    def block(columns):
        return pl.BlockSpec((strip, columns), lambda frame: (frame, 0))

    space_attn, grad_queries, own_pair, up_pair, down_pair = pl.pallas_call(
        space_attention,
        grid=(clips * frames,),
        in_specs=[
            block(3 * INNER), block(2 * INNER), block(2 * INNER), block(INNER),
            pl.BlockSpec((strip, span), lambda frame: (0, 0)),
        ],
        out_specs=[
            block(INNER), block(INNER), block(2 * INNER), block(2 * INNER), block(2 * INNER)
        ],
        out_shape=[
            jax.ShapeDtypeStruct((tokens, INNER), low),
            jax.ShapeDtypeStruct((tokens, INNER), low),
            jax.ShapeDtypeStruct((tokens, 2 * INNER), full),
            jax.ShapeDtypeStruct((tokens, 2 * INNER), low),
            jax.ShapeDtypeStruct((tokens, 2 * INNER), low),
        ],
        compiler_params=pltpu.CompilerParams(vmem_limit_bytes=VMEM_BYTES),
    )(space_qkv, before, after, space_up, table)
    from_above = passed_along(up_pair, "space", -1)
    from_below = passed_along(down_pair, "space", 1)
    space_grads, hidden_grad, hidden_low, time_up = whole_call(
        hidden_backward,
        [
            ((tokens, 3 * INNER), low), ((tokens, width), full),
            ((tokens, width), low), ((tokens, INNER), low),
        ],
        cotan, hidden, grad_queries, own_pair, from_above, from_below, space_in, time_out,
    )
    early = halved(
        by_owner(
            jnp.concatenate(
                [
                    product(cotan, space_attn),
                    product(second_in, space_grads),
                    product(hidden_low, time_attn),
                ],
                axis=1,
            )
        ),
        1,
    )
    early, placed_up = lax.optimization_barrier((early, to_places(time_up)))
    time_grads, back = whole_call(
        time_backward_here,
        [((tokens, 3 * INNER), low), ((tokens, width), low)],
        placed, time_qkv, placed_up, time_in,
    )
    late = halved(by_owner(product(first_in, time_grads)), 1)
    early, back_frames = lax.optimization_barrier((halved(early, 2), to_frames(back)))
    early = summed(early, 4)
    late = summed(late, 2)
    block_out = (hidden + dot(space_attn, space_out, 1, 1)).astype(low)
    tokens_grad = (hidden_grad + back_frames.astype(full)).astype(low)
    shape = video_tokens.shape
    return (
        block_out.reshape(shape),
        tokens_grad.reshape(shape),
        late,
        early[:, 4 * INNER :],
        early[:, INNER : 4 * INNER],
        early[:, :INNER],
    )


def solution(mesh):
    return jax.shard_map(
        shards,
        mesh=mesh,
        in_specs=(
            P("groups", "tm", "space", None),
            P("groups", "tm", "space", None),
            P(),
            P(),
            P(),
            P(),
            P(),
        ),
        out_specs=(
            P("groups", "tm", "space", None),
            P("groups", "tm", "space", None),
            P(("groups", "tm", "space"), None),
            P(("groups", "tm", "space"), None),
            P(("groups", "tm", "space"), None),
            P(("groups", "tm", "space"), None),
        ),
        check_vma=False,
    )
```

```python
import jax
import jax.numpy as jnp
from jax import lax
from jax.experimental import pallas as pl
from jax.experimental.pallas import tpu as pltpu
from jax.sharding import PartitionSpec as P

HEADS = 8
HEAD = 64
COLS = 32
INNER = HEADS * HEAD
SCALE = HEAD ** (-0.5)
EPSILON = 1e-05
VMEM_BYTES = 40 * 2**20
MASKED = -1e30


def layer_norm(values):
    center = values - jnp.mean(values, axis=-1, keepdims=True)
    variance = jnp.mean(center * center, axis=-1, keepdims=True)
    inverse = lax.rsqrt(variance + EPSILON)
    return (center * inverse, inverse)


def norm_back(normed, inverse, upstream):
    first = jnp.mean(upstream, axis=-1, keepdims=True)
    second = jnp.mean(upstream * normed, axis=-1, keepdims=True)
    return inverse * (upstream - first - normed * second)


def dot(left, right, left_dim, right_dim):
    return lax.dot_general(
        left, right, (((left_dim,), (right_dim,)), ((), ())), preferred_element_type=jnp.float32
    )


def head_of(array, index):
    return array[:, index * HEAD : (index + 1) * HEAD]


def softmax(queries, keys, allowed):
    scores = jnp.where(allowed, dot(queries * SCALE, keys, 1, 1), MASKED)
    peak = jnp.max(scores, axis=-1, keepdims=True)
    raised = jnp.exp(scores - peak)
    return raised * (1.0 / jnp.sum(raised, axis=-1, keepdims=True))


def shares_of(probs, incoming, values):
    slopes = dot(incoming, values, 1, 1)
    center = jnp.sum(probs * slopes, axis=-1, keepdims=True)
    return (probs * (slopes - center)).astype(jnp.bfloat16)


def side_by_side(members):
    return jnp.concatenate(members, axis=-1)


def same_place(tokens, places):
    rows = lax.broadcasted_iota(jnp.int32, (tokens, tokens), 0)
    columns = lax.broadcasted_iota(jnp.int32, (tokens, tokens), 1)
    return lax.rem(rows, places) == lax.rem(columns, places)


def time_forward(places, tokens_ref, weight_ref, first_ref, qkv_ref, attn_ref):
    normed, _ = layer_norm(tokens_ref[...].astype(jnp.float32))
    first = normed.astype(jnp.bfloat16)
    first_ref[...] = first
    qkv_ref[...] = dot(first, weight_ref[...], 1, 0).astype(jnp.bfloat16)
    qkv = qkv_ref[...]
    allowed = same_place(qkv.shape[0], places)
    mixed = []
    for index in range(HEADS):
        queries, keys, values = [head_of(qkv, index + part * HEADS) for part in range(3)]
        weights = softmax(queries, keys, allowed).astype(jnp.bfloat16)
        mixed.append(dot(weights, values, 1, 0).astype(jnp.bfloat16))
    attn_ref[...] = side_by_side(mixed)


def time_backward(places, tokens_ref, qkv_ref, up_ref, weight_ref, grads_ref, back_ref):
    qkv = qkv_ref[...]
    upstream = up_ref[...]
    allowed = same_place(qkv.shape[0], places)
    grads = [[], [], []]
    for index in range(HEADS):
        queries, keys, values = [head_of(qkv, index + part * HEADS) for part in range(3)]
        incoming = head_of(upstream, index)
        probs = softmax(queries, keys, allowed)
        weights = probs.astype(jnp.bfloat16)
        shares = shares_of(probs, incoming, values)
        grads[0].append((dot(shares, keys, 1, 0) * SCALE).astype(jnp.bfloat16))
        grads[1].append((dot(shares, queries, 0, 0) * SCALE).astype(jnp.bfloat16))
        grads[2].append(dot(weights, incoming, 0, 0).astype(jnp.bfloat16))
    grads_ref[...] = side_by_side(grads[0] + grads[1] + grads[2])
    normed, inverse = layer_norm(tokens_ref[...].astype(jnp.float32))
    back = dot(grads_ref[...], weight_ref[...], 1, 1)
    back_ref[...] = norm_back(normed, inverse, back).astype(jnp.bfloat16)


def space_project(tokens_ref, attn_ref, out_ref, weight_ref, hidden_ref, second_ref, qkv_ref):
    hidden = tokens_ref[...].astype(jnp.float32) + dot(attn_ref[...], out_ref[...], 1, 1)
    hidden_ref[...] = hidden
    normed, _ = layer_norm(hidden)
    second = normed.astype(jnp.bfloat16)
    second_ref[...] = second
    qkv_ref[...] = dot(second, weight_ref[...], 1, 0).astype(jnp.bfloat16)


def space_attention(
    qkv_ref, before_ref, after_ref, up_ref, table_ref, attn_ref, query_ref, own_ref, up_out, down_out
):
    strip = qkv_ref.shape[0]
    span = table_ref.shape[1]
    rows = lax.broadcasted_iota(jnp.int32, (strip, 3 * strip), 0) // COLS
    columns = lax.broadcasted_iota(jnp.int32, (strip, 3 * strip), 1) // COLS
    offsets = columns - strip // COLS - rows + (span - 1) // 2
    picked = jnp.zeros((strip, 3 * strip), jnp.float32)
    for spot in range(span):
        picked = jnp.where(offsets == spot, table_ref[:, spot : spot + 1], picked)
    allowed = picked > 0.5
    qkv = qkv_ref[...]
    upstream = up_ref[...]
    near = jnp.concatenate([before_ref[...], qkv[:, INNER:], after_ref[...]], axis=0)
    mixed, grad_queries, grad_keys, grad_values = [], [], [], []
    for index in range(HEADS):
        queries = head_of(qkv, index)
        keys = head_of(near, index)
        values = head_of(near, index + HEADS)
        incoming = head_of(upstream, index)
        probs = softmax(queries, keys, allowed)
        weights = probs.astype(jnp.bfloat16)
        mixed.append(dot(weights, values, 1, 0).astype(jnp.bfloat16))
        shares = shares_of(probs, incoming, values)
        grad_queries.append((dot(shares, keys, 1, 0) * SCALE).astype(jnp.bfloat16))
        grad_keys.append(dot(shares, queries, 0, 0) * SCALE)
        grad_values.append(dot(weights, incoming, 0, 0))
    attn_ref[...] = side_by_side(mixed)
    query_ref[...] = side_by_side(grad_queries)
    pair = side_by_side(grad_keys + grad_values)
    up_out[...] = pair[:strip].astype(jnp.bfloat16)
    own_ref[...] = pair[strip : 2 * strip]
    down_out[...] = pair[2 * strip :].astype(jnp.bfloat16)


def hidden_backward(
    cotangent_ref, hidden_ref, query_ref, own_ref, one_ref, two_ref, weight_ref, out_ref,
    grads_ref, grad_ref, low_ref, up_ref,
):
    pair = own_ref[...] + one_ref[...].astype(jnp.float32) + two_ref[...].astype(jnp.float32)
    grads = side_by_side([query_ref[...], pair.astype(jnp.bfloat16)])
    grads_ref[...] = grads
    normed, inverse = layer_norm(hidden_ref[...])
    back = norm_back(normed, inverse, dot(grads, weight_ref[...], 1, 1))
    total = cotangent_ref[...].astype(jnp.float32) + back
    grad_ref[...] = total
    low = total.astype(jnp.bfloat16)
    low_ref[...] = low
    up_ref[...] = dot(low, out_ref[...], 1, 0).astype(jnp.bfloat16)


def whole_call(body, outs, *arrays):
    return pl.pallas_call(
        body,
        out_shape=[jax.ShapeDtypeStruct(shape, kind) for shape, kind in outs],
        compiler_params=pltpu.CompilerParams(vmem_limit_bytes=VMEM_BYTES),
    )(*arrays)


def passed_along(value, axis, steps):
    count = lax.axis_size(axis)
    leading, last = (max(0, -steps), min(count, count - steps))
    return lax.ppermute(value, axis, [(source, source + steps) for source in range(leading, last)])


def product(left, right):
    return dot(left, right, 0, 0).astype(jnp.bfloat16)


def by_owner(partial):
    rows, columns = partial.shape
    times, places = lax.axis_size("tm"), lax.axis_size("space")
    return partial.reshape(times, places, rows // (times * places), columns)


def halved(held, step):
    times, left, rows, columns = held.shape
    split = held.reshape(times, left // 2, 2, rows, columns)
    bit = lax.rem(lax.axis_index("space") // step, 2)
    keep = lax.dynamic_index_in_dim(split, bit, 2, keepdims=False)
    give = lax.dynamic_index_in_dim(split, 1 - bit, 2, keepdims=False)
    pairs = [(i, i ^ step) for i in range(lax.axis_size("space"))]
    got = lax.ppermute(give, "space", pairs)
    return (keep.astype(jnp.float32) + got.astype(jnp.float32)).astype(jnp.bfloat16)


def summed(held, step):
    while held.shape[1] > 1:
        held = halved(held, step)
        step *= 2
    held = held.reshape(held.shape[0] * held.shape[2], held.shape[3])
    return lax.psum_scatter(held, "tm", scatter_dimension=0, tiled=True).astype(jnp.float32)


def shards(video_tokens, cotangent, time_in, time_out, space_in, space_out, block_mask):
    clips, frames, strip, width = video_tokens.shape
    times = lax.axis_size("tm")
    places = strip // times
    tokens = clips * frames * strip
    low, full = jnp.bfloat16, jnp.float32

    def to_places(array):
        wide = array.reshape(clips, frames, strip, array.shape[-1])
        moved = lax.all_to_all(wide, "tm", split_axis=2, concat_axis=1, tiled=True)
        return moved.reshape(tokens, array.shape[-1])

    def to_frames(array):
        wide = array.reshape(clips, frames * times, places, array.shape[-1])
        moved = lax.all_to_all(wide, "tm", split_axis=1, concat_axis=2, tiled=True)
        return moved.reshape(tokens, array.shape[-1])

    own_tokens = video_tokens.reshape(tokens, width)
    cotan = cotangent.reshape(tokens, width)
    placed = to_places(own_tokens)
    space_up = dot(cotan, space_out, 1, 0).astype(low)

    total, span = block_mask.shape
    reach = (span - 1) // 2
    rows_dev = strip // COLS
    first_row = lax.axis_index("space") * rows_dev
    own_mask = lax.dynamic_slice_in_dim(block_mask, first_row, rows_dev, axis=0)
    spots = jnp.arange(span, dtype=jnp.int32)[None, :] - reach
    key_rows = first_row + jnp.arange(rows_dev, dtype=jnp.int32)[:, None] + spots
    table = ((own_mask == 1) | (spots == 0)) & (key_rows >= 0) & (key_rows < total)
    table = jnp.repeat(table.astype(full), COLS, axis=0)

    def time_forward_here(*refs):
        time_forward(places, *refs)

    def time_backward_here(*refs):
        time_backward(places, *refs)

    first_in, time_qkv, mixed = whole_call(
        time_forward_here,
        [((tokens, width), low), ((tokens, 3 * INNER), low), ((tokens, INNER), low)],
        placed, time_in,
    )
    time_attn = to_frames(mixed)
    hidden, second_in, space_qkv = whole_call(
        space_project,
        [((tokens, width), full), ((tokens, width), low), ((tokens, 3 * INNER), low)],
        own_tokens, time_attn, time_out, space_in,
    )
    pair = space_qkv[:, INNER:]
    before = passed_along(pair, "space", 1)
    after = passed_along(pair, "space", -1)

    def block(columns):
        return pl.BlockSpec((strip, columns), lambda frame: (frame, 0))

    space_attn, grad_queries, own_pair, up_pair, down_pair = pl.pallas_call(
        space_attention,
        grid=(clips * frames,),
        in_specs=[
            block(3 * INNER), block(2 * INNER), block(2 * INNER), block(INNER),
            pl.BlockSpec((strip, span), lambda frame: (0, 0)),
        ],
        out_specs=[
            block(INNER), block(INNER), block(2 * INNER), block(2 * INNER), block(2 * INNER)
        ],
        out_shape=[
            jax.ShapeDtypeStruct((tokens, INNER), low),
            jax.ShapeDtypeStruct((tokens, INNER), low),
            jax.ShapeDtypeStruct((tokens, 2 * INNER), full),
            jax.ShapeDtypeStruct((tokens, 2 * INNER), low),
            jax.ShapeDtypeStruct((tokens, 2 * INNER), low),
        ],
        compiler_params=pltpu.CompilerParams(vmem_limit_bytes=VMEM_BYTES),
    )(space_qkv, before, after, space_up, table)
    from_above = passed_along(up_pair, "space", -1)
    from_below = passed_along(down_pair, "space", 1)
    space_grads, hidden_grad, hidden_low, time_up = whole_call(
        hidden_backward,
        [
            ((tokens, 3 * INNER), low), ((tokens, width), full),
            ((tokens, width), low), ((tokens, INNER), low),
        ],
        cotan, hidden, grad_queries, own_pair, from_above, from_below, space_in, time_out,
    )
    early = halved(
        by_owner(
            jnp.concatenate(
                [
                    product(cotan, space_attn),
                    product(second_in, space_grads),
                    product(hidden_low, time_attn),
                ],
                axis=1,
            )
        ),
        1,
    )
    early, placed_up = lax.optimization_barrier((early, to_places(time_up)))
    time_grads, back = whole_call(
        time_backward_here,
        [((tokens, 3 * INNER), low), ((tokens, width), low)],
        placed, time_qkv, placed_up, time_in,
    )
    late = halved(by_owner(product(first_in, time_grads)), 1)
    early, back_frames = lax.optimization_barrier((halved(early, 2), to_frames(back)))
    early = summed(early, 4)
    while late.shape[1] > 1:
        late = halved(late, lax.axis_size("space") // late.shape[1])
    pieces = lax.all_to_all(late[:, 0], "tm", split_axis=0, concat_axis=0, tiled=True)
    late = jnp.sum(pieces.astype(full), axis=0)
    block_out = (hidden + dot(space_attn, space_out, 1, 1)).astype(low)
    tokens_grad = (hidden_grad + back_frames.astype(full)).astype(low)
    shape = video_tokens.shape
    return (
        block_out.reshape(shape),
        tokens_grad.reshape(shape),
        late,
        early[:, 4 * INNER :],
        early[:, INNER : 4 * INNER],
        early[:, :INNER],
    )


def solution(mesh):
    return jax.shard_map(
        shards,
        mesh=mesh,
        in_specs=(
            P("groups", "tm", "space", None),
            P("groups", "tm", "space", None),
            P(),
            P(),
            P(),
            P(),
            P(),
        ),
        out_specs=(
            P("groups", "tm", "space", None),
            P("groups", "tm", "space", None),
            P(("groups", "tm", "space"), None),
            P(("groups", "tm", "space"), None),
            P(("groups", "tm", "space"), None),
            P(("groups", "tm", "space"), None),
        ),
        check_vma=False,
    )
```
